32 devices in a mesh: replica: 2 (over y), expert: 16 (over z, x, core).
Axes of the slice: x: 2, y: 2, z: 4, core: 2. Of those that a mesh axis runs over, the one named last changes fastest.
Arguments:
- hidden_in: bfloat16 [2, 128, 7168], P(None, ('replica', 'expert')), parts along dimension 1, may hold values from -6 to 6
- norm_gain: float32 [7168], replicated, may hold values from 0.25 to 1.75
- router: float32 [7168, 8], replicated, may hold values from -0.0625 to 0.0625
- expert_ids: int32 [2, 128, 2], P(None, ('replica', 'expert')), parts along dimension 1, may hold values from 0 to 7, all different within a row; in each aligned block of 4 rows (0 to 3, 4 to 7, ..., all dimensions but the last counted through in order) at most 2 rows name the same one
- w_gate: bfloat16 [16, 7168, 1024], P('expert'), may hold values from -0.0625 to 0.0625
- w_up: bfloat16 [16, 7168, 1024], P('expert'), may hold values from -0.0625 to 0.0625
- w_down: bfloat16 [16, 1024, 7168], P('expert'), may hold values from -0.125 to 0.125
Outputs:
- hidden_out: bfloat16 [2, 128, 7168], P(None, ('replica', 'expert')), parts along dimension 1
The draws below stay inside these ranges and needn't reach their ends.
There are 2 independent parts, one for each index of `replica`. The reference program is written for one: setup_inputs(seed, part) draws one part's arguments, and reference() takes and returns one part's arrays. A program takes and returns all parts, laid end to end along the dimension named above; an argument that names none is the same for every part. Nothing has to cross between parts.
Inputs may be any that keep to these rules, and one draw needn't show every extreme that they name: `expert_ids`: each row names 2 different experts; among the 4 tokens of one device and one micro-batch no expert is named more than 2 times, a bound that some block reaches.
All inputs are finite; a program needn't handle non-finite values.
Results may differ from the reference program's by a relative error of at most 0.0063.
Values may be sent and summed in bfloat16 or wider, within the bound.
A program may use at most 128 MiB of HBM per device.

```python
import math
import jax
import jax.numpy as jnp
import numpy as np
from jax import lax

D = 7168
FF = 2048
EXPERTS = 8
TOPK = 2
MB = 2
TOK_DEV = 4
CAP = 2
GROUP = 2
FF_DEV = 1024
TOKENS = 64
N_EXPERT = 16


def steps_of(rng, shape, cuts, low, high):
    gain = 1.0
    for axis_at, blocks in cuts:
        draws = jax.random.uniform(jax.random.fold_in(jax.random.fold_in(rng, 6), axis_at), (blocks,), jnp.float32, low / len(cuts), high / len(cuts))
        gain = gain * jnp.repeat(jnp.exp(draws), shape[axis_at] // blocks).reshape((-1,) + (1,) * (len(shape) - 1 - axis_at))
    return gain


def shared_out(rng, own, number, rows, number_of, top, reach, skew):
    order = jax.random.permutation(rng, number_of)
    heavy_load, usual = load_shares(number_of, rows * top, reach, skew, True), load_shares(number_of, rows * top, reach, skew, False)
    places = jnp.arange(number_of)

    def named(tallies, turn):
        used = int((tallies > 0).sum())
        fixed = max(1, used // 4)
        shifted = fixed + (places - fixed + turn * (used - fixed)) % max(1, number_of - fixed)
        return jnp.zeros((number_of,), jnp.int32).at[order[jnp.where(places < fixed, places, shifted)]].set(jnp.asarray(tallies, jnp.int32))

    tallies = jnp.where(number % 4 == 0, named(heavy_load, number // 4), named(usual, number - number // 4 - 1))
    mixed = jax.random.permutation(jax.random.fold_in(own, 3), number_of)
    giver, sink = mixed[0:number_of // 2 * 2:2], mixed[1:number_of // 2 * 2:2]
    margin = jnp.minimum(tallies[giver] - 1, reach - tallies[sink]) // 2
    margin = jnp.where((giver == order[0]) | (sink == order[0]) | (tallies[sink] == 0), 0, jnp.maximum(margin, 0))
    shifted = jax.random.randint(jax.random.fold_in(own, 4), (number_of // 2,), 0, 1 << 20) % (margin + 1)
    tallies = tallies.at[giver].add(-shifted).at[sink].add(shifted)
    items = jnp.searchsorted(jnp.cumsum(tallies), jnp.arange(rows * top), side="right").astype(jnp.int32)
    grid = items.reshape(top, rows).T
    grid = grid[jax.random.permutation(jax.random.fold_in(own, 1), rows)]
    turn = jax.random.randint(jax.random.fold_in(own, 2), (rows, 1), 0, top)
    return jnp.take_along_axis(grid, (jnp.arange(top)[None, :] + turn) % top, axis=1)


def load_shares(number_of, total, limit, skew, full):
    weights = [(1 << 20) // math.isqrt(rank ** skew) + 1 for rank in range(1, number_of + 1)]
    largest = limit if full else min(limit, max(-(-total // number_of), total * weights[0] // sum(weights)))
    least = 1 if total - largest >= number_of - 1 else 0
    given, spare = [largest] + [least] * (number_of - 1), total - largest - least * (number_of - 1)
    while spare > 0:
        candidates = [i for i in range(1, number_of) if given[i] < largest] or [i for i in range(1, number_of) if given[i] < limit]
        mass, budget = sum([weights[i] for i in candidates]), spare
        for i in candidates:
            extra = min(limit - given[i], max(1, budget * weights[i] // mass), spare)
            given[i] = given[i] + extra
            spare = spare - extra
    return np.array(given)


def bell_draw(key, dims, spread, limit, shards=(), kind=jnp.bfloat16):
    array = spread * jax.random.normal(key, dims, jnp.float32)
    if shards:
        array = array * steps_of(key, dims, shards, -0.22, 0.18)
    return jnp.clip(array, -limit, limit).astype(kind)


def setup_inputs(seed: int = 0, part: int = 0) -> dict:
    seeds = jax.random.split(jax.random.key(seed), 8)
    part_keys = jax.random.split(jax.random.fold_in(seeds[7], part), 8)
    hidden_in = bell_draw(part_keys[0], (MB, TOKENS, D), 1.0, 6.0, ((1, 16),))
    norm_gain = jnp.clip(1.0 + 0.15 * jax.random.normal(seeds[1], (D,), jnp.float32), 0.25, 1.75)
    router = bell_draw(seeds[2], (D, EXPERTS), D ** -0.5, 0.0625, (), jnp.float32)
    expert_ids_keys = jax.random.split(jax.random.fold_in(part_keys[3], 1), MB * TOKENS // TOK_DEV)
    expert_ids_turns = jax.random.permutation(jax.random.fold_in(part_keys[3], 3), MB * TOKENS // TOK_DEV)
    expert_ids = jax.vmap(lambda own, number: shared_out(jax.random.fold_in(part_keys[3], 2), own, number, TOK_DEV, EXPERTS, TOPK, CAP, 2))(expert_ids_keys, expert_ids_turns).reshape((MB, TOKENS, TOPK))
    w_gate = bell_draw(seeds[4], (N_EXPERT, D, FF_DEV), D ** -0.5, 0.0625, ((0, 16),))
    w_up = bell_draw(seeds[5], (N_EXPERT, D, FF_DEV), D ** -0.5, 0.0625, ((0, 16),))
    w_down = bell_draw(seeds[6], (N_EXPERT, FF_DEV, D), FF ** -0.5, 0.125, ((0, 16),))
    return {"hidden_in": hidden_in, "norm_gain": norm_gain, "router": router, "expert_ids": expert_ids, "w_gate": w_gate, "w_up": w_up, "w_down": w_down}


def reference(hidden_in, norm_gain, router, expert_ids, w_gate, w_up, w_down):
    gate_all = w_gate.reshape(EXPERTS, GROUP, D, FF_DEV)
    up_all = w_up.reshape(EXPERTS, GROUP, D, FF_DEV)
    down_all = w_down.reshape(EXPERTS, GROUP, FF_DEV, D)
    slots = N_EXPERT * CAP
    results = []
    for micro in range(MB):
        stream = hidden_in[micro].astype(jnp.float32)
        normed = stream * lax.rsqrt(lax.optimization_barrier(jnp.mean(stream * stream, axis=-1, keepdims=True)) + 1e-06) * norm_gain
        dispatched = normed.astype(jnp.bfloat16)
        scores = jax.nn.sigmoid(jnp.dot(normed, router, precision=lax.Precision.HIGHEST))
        routed_ids = expert_ids[micro]
        chosen = jnp.take_along_axis(scores, routed_ids, axis=1)
        gates = 2.5 * chosen / lax.optimization_barrier(jnp.sum(chosen, axis=1, keepdims=True))
        table = lax.optimization_barrier(jnp.sum(gates[:, :, None] * (routed_ids[:, :, None] == jnp.arange(EXPERTS, dtype=jnp.int32)).astype(jnp.float32), axis=1))

        def add_expert(expert, total):
            routed = jnp.any(routed_ids == expert, axis=1)
            count = jnp.sum(routed.astype(jnp.int32))
            index = jnp.nonzero(routed, size=slots, fill_value=0)[0].astype(jnp.int32)
            valid = (jnp.arange(slots, dtype=jnp.int32) < count).astype(jnp.float32)
            rows = dispatched[index]
            gate_mat = gate_all[expert].transpose(1, 0, 2).reshape(D, FF)
            up_mat = up_all[expert].transpose(1, 0, 2).reshape(D, FF)
            gated = jnp.dot(rows, gate_mat, preferred_element_type=jnp.float32)
            upper = jnp.dot(rows, up_mat, preferred_element_type=jnp.float32)
            inner = (jax.nn.silu(gated) * upper).astype(jnp.bfloat16)
            pieces = jnp.einsum('rsf,sfd->rsd', inner.reshape(slots, GROUP, FF_DEV).astype(jnp.float32), down_all[expert].astype(jnp.float32))
            pieces = lax.optimization_barrier(pieces.astype(jnp.bfloat16))
            expert_out = lax.optimization_barrier(jnp.sum(pieces.astype(jnp.float32), axis=1))
            weight = table[index, expert] * valid
            return total.at[index].add(weight[:, None] * expert_out)
        mixed = lax.fori_loop(0, EXPERTS, add_expert, jnp.zeros((TOKENS, D), jnp.float32))
        results.append((stream + mixed).astype(jnp.bfloat16))
    return jnp.stack(results, axis=0)
```

```python
import functools

import jax
import jax.numpy as jnp
from jax import lax
from jax.experimental import pallas as pl
from jax.experimental.pallas import tpu as pltpu
from jax.sharding import PartitionSpec as P

EXPERTS = 8
PACK = 4
ROWS = 16
SENDERS = 16
F32 = jnp.float32
BF16 = jnp.bfloat16


def dot(a, b, precision=None):
    return jnp.dot(a, b, preferred_element_type=F32, precision=precision)


def iota(shape, dim):
    return lax.broadcasted_iota(jnp.int32, shape, dim)


def kernel(
    n,
    pieces,
    hid,
    gain,
    router,
    ids,
    wg_hbm,
    wu_hbm,
    wd_hbm,
    out,
    wg,
    wu,
    wd,
    stream,
    normed,
    outbox,
    arr,
    xs,
    perm,
    gate_acc,
    up_acc,
    inner,
    ysend,
    yrecv,
    ystack,
    packed,
    back,
    gated_place,
    w_sem,
    d_send,
    d_recv,
    f_send,
    f_recv,
    y_send,
    y_recv,
    b_send,
    b_recv,
):
    me = lax.axis_index("expert")
    core = lax.rem(me, 2)
    other = 1 - core
    partner = me + 1 - 2 * core
    group = n // EXPERTS
    pairs = group // 2
    width = hid.shape[2]
    half = width // 2
    quarter = half // PACK
    rows = n * 4
    blocks = n // SENDERS

    def weight_copy(src, dst, h, sem):
        at = pl.ds(pl.multiple_of(h * half, 128), half)
        return pltpu.make_async_copy(src.at[0, at, :], dst.at[at, :], w_sem.at[sem])

    copies = [
        weight_copy(wg_hbm, wg, core, 0),
        weight_copy(wu_hbm, wu, core, 1),
        weight_copy(wg_hbm, wg, other, 2),
        weight_copy(wu_hbm, wu, other, 3),
        pltpu.make_async_copy(wd_hbm.at[0], wd, w_sem.at[4]),
    ]
    for copy in copies:
        copy.start()

    barrier = pltpu.get_barrier_semaphore()

    def greet(i, _):
        pl.semaphore_signal(
            barrier,
            inc=1,
            device_id={"expert": lax.rem(me + i, n)},
            device_id_type=pl.DeviceIdType.MESH,
        )
        return 0

    lax.fori_loop(1, n, greet, 0)

    x = jnp.concatenate([hid[0].astype(F32), hid[1].astype(F32)], axis=0)
    stream[...] = x
    scale = lax.rsqrt(jnp.mean(x * x, axis=-1, keepdims=True) + 1e-06)
    y = x * scale * gain[...]
    normed[...] = y

    diagonal = iota((4, 4), 0) == iota((4, 4), 1)

    def choice(k):
        return jnp.concatenate(
            [
                jnp.sum(
                    jnp.where(diagonal, ids[m, k : k + 1, :].astype(F32), 0.0),
                    axis=1,
                    keepdims=True,
                )
                for m in range(2)
            ],
            axis=0,
        )

    col = iota((8, 128), 1)
    expert = (col // ROWS).astype(F32)
    member = jnp.where((choice(0) == expert) | (choice(1) == expert), 1.0, 0.0).astype(F32)
    r8, c8 = iota((8, 8), 0), iota((8, 8), 1)
    earlier = jnp.where((c8 < r8) & (c8 // 4 == r8 // 4), 1.0, 0.0).astype(F32)
    position = dot(earlier, member)
    token = iota((8, 128), 0)
    slot = lax.rem(col, 4) - 2 * (token // 4)
    place = jnp.where(position == slot.astype(F32), member, 0.0)
    piece = lax.rem(col // 4, PACK)
    spread = jnp.concatenate([jnp.where(piece == c, place, 0.0) for c in range(PACK)], axis=0)
    spread_t = spread.T.astype(BF16)
    for h in range(2):
        stack = jnp.concatenate(
            [
                normed[:, h * half + c * quarter : h * half + (c + 1) * quarter]
                for c in range(PACK)
            ],
            axis=0,
        ).astype(BF16)
        outbox[h] = dot(spread_t, stack).astype(BF16)

    pl.semaphore_wait(barrier, n - 1)

    def remote(src, dst, send, recv, target):
        return pltpu.make_async_remote_copy(
            src_ref=src,
            dst_ref=dst,
            send_sem=send,
            recv_sem=recv,
            device_id={"expert": target},
            device_id_type=pl.DeviceIdType.MESH,
        )

    def at16(index):
        return pl.ds(pl.multiple_of(index * ROWS, ROWS), ROWS)

    for p, (off, w) in enumerate(pieces):
        lanes = pl.ds(off, w)

        def dispatch(i, _):
            target = lax.rem(me + i, n)
            h = lax.rem(target, 2)
            remote(
                outbox.at[h, at16(target // group), lanes],
                arr.at[h, at16(me), lanes],
                d_send.at[p],
                d_recv.at[p],
                target,
            ).start()
            return 0

        lax.fori_loop(1, n, dispatch, 0)
    arr[core, at16(me), :] = outbox[core, at16(me // group), :]

    logits = lax.dot_general(
        normed[...],
        router[...],
        (((1,), (1,)), ((), ())),
        precision=lax.Precision.HIGHEST,
        preferred_element_type=F32,
    )
    scores = jax.nn.sigmoid(logits)
    widen = jnp.where(iota((8, 128), 0) == iota((8, 128), 1) // ROWS, 1.0, 0.0).astype(F32)
    wide = dot(scores, widen, lax.Precision.HIGHEST) * member
    gates = 2.5 * wide / (jnp.sum(wide, axis=1, keepdims=True) * (1.0 / ROWS))
    gated = spread * jnp.concatenate([gates] * PACK, axis=0)
    high = gated.astype(BF16)
    gated_place[0:32, :] = high
    gated_place[32:64, :] = (gated - high.astype(F32)).astype(BF16)

    span = SENDERS * ROWS
    r, q = iota((span, span), 0), iota((span, span), 1)

    def where_from(v):
        return lax.rem(v, 64) // 4 * ROWS + v // 64 * 4 + lax.rem(v, 4)

    perm[0] = jnp.where(where_from(r) == q, 1.0, 0.0).astype(BF16)
    perm[1] = jnp.where(where_from(q) == r, 1.0, 0.0).astype(BF16)
    gate_acc[...] = jnp.zeros_like(gate_acc)
    up_acc[...] = jnp.zeros_like(up_acc)

    def hidden_units(h, off, w):
        lanes = pl.ds(off, w)

        def unpack(b, _):
            z = dot(perm[0], arr[h, pl.ds(pl.multiple_of(b * span, span), span), lanes])
            z = z.astype(BF16)
            for c in range(PACK):
                xs[c, pl.ds(pl.multiple_of(b * 64, 64), 64), 0:w] = z[c * 64 : c * 64 + 64]
            return 0

        lax.fori_loop(0, blocks, unpack, 0)

        def add(c, _):
            depth = pl.ds(pl.multiple_of(h * half + c * quarter + off, 128), w)
            part = xs[c, :, 0:w]
            gate_acc[...] += dot(part, wg[depth, :])
            up_acc[...] += dot(part, wu[depth, :])
            return 0

        lax.fori_loop(0, PACK, add, 0)

    def all_rows(ref, off, w, sem):
        at = ref.at[pl.ds(0, (n - 1) * ROWS), pl.ds(off, w)]
        return pltpu.make_async_copy(at, at, sem)

    def forward(p):
        off, w = pieces[p]
        at = arr.at[core, :, pl.ds(off, w)]
        return remote(at, at, f_send.at[p], f_recv.at[p], partner)

    last = len(pieces) - 1
    for p, (off, w) in enumerate(pieces):
        all_rows(packed, off, w, d_recv.at[p]).wait()
        forward(p).start()
        if p == 0:
            copies[0].wait()
            copies[1].wait()
        hidden_units(core, off, w)
    for p, (off, w) in enumerate(pieces):
        forward(p).wait_recv()
        if p == 0:
            copies[2].wait()
            copies[3].wait()
        hidden_units(other, off, w)

    g = gate_acc[...]
    inner[...] = (g / (1.0 + jnp.exp(-g)) * up_acc[...]).astype(BF16)
    copies[4].wait()

    def down(h, c, off, w):
        at = pl.ds(pl.multiple_of(h * half + c * quarter + off, 128), w)
        return dot(inner[...], wd[:, at])

    def some_rows(c):
        return pl.ds(pl.multiple_of(c * rows, 64), rows)

    def swap(p):
        off, w = pieces[p]
        lanes = pl.ds(off, w)
        return remote(
            ysend.at[:, lanes], yrecv.at[:, lanes], y_send.at[p], y_recv.at[p], partner
        )

    for p, (off, w) in enumerate(pieces):

        def give(c, _):
            ysend[some_rows(c), pl.ds(off, w)] = down(other, c, off, w).astype(BF16)
            return 0

        lax.fori_loop(0, PACK, give, 0)
        swap(p).start()

    mine = core * pairs + lax.rem(me // 2, pairs)
    home = mine * EXPERTS + me // group
    for p, (off, w) in enumerate(pieces):
        lanes = pl.ds(off, w)
        swap(p).wait_recv()

        def keep(c, _):
            at = some_rows(c)
            total = down(core, c, off, w).astype(BF16).astype(F32) + yrecv[at, lanes].astype(F32)
            ystack[at, lanes] = total.astype(BF16)
            return 0

        lax.fori_loop(0, PACK, keep, 0)

        def pack(b, _):
            stack = jnp.concatenate(
                [
                    ystack[pl.ds(pl.multiple_of(c * rows + b * 64, 64), 64), lanes]
                    for c in range(PACK)
                ],
                axis=0,
            )
            packed[pl.ds(pl.multiple_of(b * span, span), span), lanes] = dot(
                perm[1], stack
            ).astype(BF16)
            return 0

        lax.fori_loop(0, blocks, pack, 0)

        def give_back(i, _):
            target = lax.rem(me + i, n)
            remote(
                packed.at[at16(target), lanes],
                back.at[at16(home), lanes],
                b_send.at[p],
                b_recv.at[p],
                target,
            ).start()
            return 0

        lax.fori_loop(1, n, give_back, 0)
        back[at16(home), lanes] = packed[at16(me), lanes]

    for p, (off, w) in enumerate(pieces):
        all_rows(packed, off, w, b_recv.at[p]).wait()
        for h in range(2):
            total = jnp.zeros((64, w), F32)
            for k in range(pairs):
                start = (h * pairs + k) * EXPERTS * ROWS
                total += dot(gated_place[...], back[start : start + EXPERTS * ROWS, off : off + w])
            total = total[0:32] + total[32:64]
            for c in range(PACK):
                start = h * half + c * quarter + off
                value = stream[:, start : start + w] + total[c * 8 : c * 8 + 8]
                value = value.astype(BF16)
                out[0, :, start : start + w] = value[0:4]
                out[1, :, start : start + w] = value[4:8]

    for p, (off, w) in enumerate(pieces):
        all_rows(packed, off, w, d_send.at[p]).wait()
        forward(p).wait_send()
        swap(p).wait_send()
        all_rows(packed, off, w, b_send.at[p]).wait()


def on_device(hidden_in, norm_gain, router, expert_ids, w_gate, w_up, w_down):
    n = lax.axis_size("expert")
    width = hidden_in.shape[2]
    units = w_gate.shape[2]
    quarter = width // 2 // PACK
    first = (quarter // 128 + 1) // 2 * 128
    pieces = ((0, first), (first, quarter - first))
    rows = n * 4
    vmem = pl.BlockSpec(memory_space=pltpu.VMEM)
    hbm = pl.BlockSpec(memory_space=pl.ANY)
    sems = pltpu.SemaphoreType.DMA((len(pieces),))
    return pl.pallas_call(
        functools.partial(kernel, n, pieces),
        out_shape=jax.ShapeDtypeStruct(hidden_in.shape, BF16),
        in_specs=[vmem] * 4 + [hbm] * 3,
        out_specs=vmem,
        scratch_shapes=[
            pltpu.VMEM((width, units), BF16),
            pltpu.VMEM((width, units), BF16),
            pltpu.VMEM((units, width), BF16),
            pltpu.VMEM((8, width), F32),
            pltpu.VMEM((8, width), F32),
            pltpu.VMEM((2, EXPERTS * ROWS, quarter), BF16),
            pltpu.VMEM((2, n * ROWS, quarter), BF16),
            pltpu.VMEM((PACK, rows, first), BF16),
            pltpu.VMEM((2, SENDERS * ROWS, SENDERS * ROWS), BF16),
            pltpu.VMEM((rows, units), F32),
            pltpu.VMEM((rows, units), F32),
            pltpu.VMEM((rows, units), BF16),
            pltpu.VMEM((PACK * rows, quarter), BF16),
            pltpu.VMEM((PACK * rows, quarter), BF16),
            pltpu.VMEM((PACK * rows, quarter), BF16),
            pltpu.VMEM((n * ROWS, quarter), BF16),
            pltpu.VMEM((n * ROWS, quarter), BF16),
            pltpu.VMEM((64, EXPERTS * ROWS), BF16),
            pltpu.SemaphoreType.DMA((5,)),
        ]
        + [sems] * 8,
        compiler_params=pltpu.CompilerParams(
            collective_id=0, has_side_effects=True, vmem_limit_bytes=60 * 2**20
        ),
    )(
        hidden_in,
        norm_gain.reshape(1, width),
        router.T,
        expert_ids.transpose(0, 2, 1),
        w_gate,
        w_up,
        w_down,
    )


def solution(mesh):
    placed = (
        P(None, ("replica", "expert"), None),
        P(),
        P(),
        P(None, ("replica", "expert"), None),
        P("expert", None, None),
        P("expert", None, None),
        P("expert", None, None),
    )
    return jax.shard_map(
        on_device,
        mesh=mesh,
        in_specs=placed,
        out_specs=P(None, ("replica", "expert"), None),
        check_vma=False,
    )
```

```python
import functools

import jax
import jax.numpy as jnp
from jax import lax
from jax.experimental import pallas as pl
from jax.experimental.pallas import tpu as pltpu
from jax.sharding import PartitionSpec as P

EXPERTS = 8
PACK = 4
ROWS = 16
SENDERS = 16
DISPATCH = (4, 3)
RETURN = (2, 2, 3)
F32 = jnp.float32
BF16 = jnp.bfloat16


def cut(columns, shares):
    units, total = columns // 128, sum(shares)
    ends = [units * sum(shares[: k + 1]) // total * 128 for k in range(len(shares))]
    starts = [0] + ends[:-1]
    return tuple((a, b - a) for a, b in zip(starts, ends) if b > a)


def dot(a, b, precision=None):
    return jnp.dot(a, b, preferred_element_type=F32, precision=precision)


def iota(shape, dim):
    return lax.broadcasted_iota(jnp.int32, shape, dim)


def kernel(
    n,
    pieces,
    returns,
    hid,
    gain,
    router,
    ids,
    wg_hbm,
    wu_hbm,
    wd_hbm,
    out,
    wg,
    wu,
    wd,
    stream,
    normed,
    outbox,
    arr,
    xs,
    perm,
    gate_acc,
    up_acc,
    inner,
    ysend,
    yrecv,
    ystack,
    packed,
    back,
    gated_place,
    w_sem,
    d_send,
    d_recv,
    f_send,
    f_recv,
    y_send,
    y_recv,
    b_send,
    b_recv,
):
    me = lax.axis_index("expert")
    core = lax.rem(me, 2)
    other = 1 - core
    partner = me + 1 - 2 * core
    group = n // EXPERTS
    pairs = group // 2
    width = hid.shape[2]
    half = width // 2
    quarter = half // PACK
    rows = n * 4
    blocks = n // SENDERS

    def weight_copy(src, dst, h, sem):
        at = pl.ds(pl.multiple_of(h * half, 128), half)
        return pltpu.make_async_copy(src.at[0, at, :], dst.at[at, :], w_sem.at[sem])

    copies = [
        weight_copy(wg_hbm, wg, core, 0),
        weight_copy(wu_hbm, wu, core, 1),
        weight_copy(wg_hbm, wg, other, 2),
        weight_copy(wu_hbm, wu, other, 3),
        pltpu.make_async_copy(wd_hbm.at[0], wd, w_sem.at[4]),
    ]
    for copy in copies:
        copy.start()

    barrier = pltpu.get_barrier_semaphore()

    def greet(i, _):
        pl.semaphore_signal(
            barrier,
            inc=1,
            device_id={"expert": lax.rem(me + i, n)},
            device_id_type=pl.DeviceIdType.MESH,
        )
        return 0

    lax.fori_loop(1, n, greet, 0)

    x = jnp.concatenate([hid[0].astype(F32), hid[1].astype(F32)], axis=0)
    stream[...] = x
    scale = lax.rsqrt(jnp.mean(x * x, axis=-1, keepdims=True) + 1e-06)
    y = x * scale * gain[...]
    normed[...] = y

    diagonal = iota((4, 4), 0) == iota((4, 4), 1)

    def choice(k):
        return jnp.concatenate(
            [
                jnp.sum(
                    jnp.where(diagonal, ids[m, k : k + 1, :].astype(F32), 0.0),
                    axis=1,
                    keepdims=True,
                )
                for m in range(2)
            ],
            axis=0,
        )

    col = iota((8, 128), 1)
    expert = (col // ROWS).astype(F32)
    member = jnp.where((choice(0) == expert) | (choice(1) == expert), 1.0, 0.0).astype(F32)
    r8, c8 = iota((8, 8), 0), iota((8, 8), 1)
    earlier = jnp.where((c8 < r8) & (c8 // 4 == r8 // 4), 1.0, 0.0).astype(F32)
    position = dot(earlier, member)
    token = iota((8, 128), 0)
    slot = lax.rem(col, 4) - 2 * (token // 4)
    place = jnp.where(position == slot.astype(F32), member, 0.0)
    piece = lax.rem(col // 4, PACK)
    spread = jnp.concatenate([jnp.where(piece == c, place, 0.0) for c in range(PACK)], axis=0)
    spread_t = spread.T.astype(BF16)
    for h in range(2):
        stack = jnp.concatenate(
            [
                normed[:, h * half + c * quarter : h * half + (c + 1) * quarter]
                for c in range(PACK)
            ],
            axis=0,
        ).astype(BF16)
        outbox[h] = dot(spread_t, stack).astype(BF16)

    pl.semaphore_wait(barrier, n - 1)

    def remote(src, dst, send, recv, target):
        return pltpu.make_async_remote_copy(
            src_ref=src,
            dst_ref=dst,
            send_sem=send,
            recv_sem=recv,
            device_id={"expert": target},
            device_id_type=pl.DeviceIdType.MESH,
        )

    def at16(index):
        return pl.ds(pl.multiple_of(index * ROWS, ROWS), ROWS)

    for p, (off, w) in enumerate(pieces):
        lanes = pl.ds(off, w)

        def dispatch(i, _):
            target = lax.rem(me + i, n)
            h = lax.rem(target, 2)
            remote(
                outbox.at[h, at16(target // group), lanes],
                arr.at[h, at16(me), lanes],
                d_send.at[p],
                d_recv.at[p],
                target,
            ).start()
            return 0

        lax.fori_loop(1, n, dispatch, 0)
    arr[core, at16(me), :] = outbox[core, at16(me // group), :]

    logits = lax.dot_general(
        normed[...],
        router[...],
        (((1,), (1,)), ((), ())),
        precision=lax.Precision.HIGHEST,
        preferred_element_type=F32,
    )
    scores = jax.nn.sigmoid(logits)
    widen = jnp.where(iota((8, 128), 0) == iota((8, 128), 1) // ROWS, 1.0, 0.0).astype(F32)
    wide = dot(scores, widen, lax.Precision.HIGHEST) * member
    gates = 2.5 * wide / (jnp.sum(wide, axis=1, keepdims=True) * (1.0 / ROWS))
    gated = spread * jnp.concatenate([gates] * PACK, axis=0)
    high = gated.astype(BF16)
    gated_place[0:32, :] = high
    gated_place[32:64, :] = (gated - high.astype(F32)).astype(BF16)

    span = SENDERS * ROWS
    r, q = iota((span, span), 0), iota((span, span), 1)

    def where_from(v):
        return lax.rem(v, 64) // 4 * ROWS + v // 64 * 4 + lax.rem(v, 4)

    perm[0] = jnp.where(where_from(r) == q, 1.0, 0.0).astype(BF16)
    perm[1] = jnp.where(where_from(q) == r, 1.0, 0.0).astype(BF16)
    gate_acc[...] = jnp.zeros_like(gate_acc)
    up_acc[...] = jnp.zeros_like(up_acc)

    def hidden_units(h, off, w):
        lanes = pl.ds(off, w)

        def unpack(b, _):
            z = dot(perm[0], arr[h, pl.ds(pl.multiple_of(b * span, span), span), lanes])
            z = z.astype(BF16)
            for c in range(PACK):
                xs[c, pl.ds(pl.multiple_of(b * 64, 64), 64), 0:w] = z[c * 64 : c * 64 + 64]
            return 0

        lax.fori_loop(0, blocks, unpack, 0)

        def add(c, _):
            depth = pl.ds(pl.multiple_of(h * half + c * quarter + off, 128), w)
            part = xs[c, :, 0:w]
            gate_acc[...] += dot(part, wg[depth, :])
            up_acc[...] += dot(part, wu[depth, :])
            return 0

        lax.fori_loop(0, PACK, add, 0)

    def all_rows(ref, off, w, sem):
        at = ref.at[pl.ds(0, (n - 1) * ROWS), pl.ds(off, w)]
        return pltpu.make_async_copy(at, at, sem)

    def forward(p):
        off, w = pieces[p]
        at = arr.at[core, :, pl.ds(off, w)]
        return remote(at, at, f_send.at[p], f_recv.at[p], partner)

    for p, (off, w) in enumerate(pieces):
        all_rows(packed, off, w, d_recv.at[p]).wait()
        forward(p).start()
        if p == 0:
            copies[0].wait()
            copies[1].wait()
        hidden_units(core, off, w)
        forward(p).wait_recv()
        if p == 0:
            copies[2].wait()
            copies[3].wait()
        hidden_units(other, off, w)

    g = gate_acc[...]
    inner[...] = (g / (1.0 + jnp.exp(-g)) * up_acc[...]).astype(BF16)
    copies[4].wait()

    def down(h, c, off, w):
        at = pl.ds(pl.multiple_of(h * half + c * quarter + off, 128), w)
        return dot(inner[...], wd[:, at])

    def some_rows(c):
        return pl.ds(pl.multiple_of(c * rows, 64), rows)

    def swap(p):
        off, w = returns[p]
        lanes = pl.ds(off, w)
        return remote(
            ysend.at[:, lanes], yrecv.at[:, lanes], y_send.at[p], y_recv.at[p], partner
        )

    def give_piece(p):
        off, w = returns[p]

        def give(c, _):
            ysend[some_rows(c), pl.ds(off, w)] = down(other, c, off, w).astype(BF16)
            return 0

        lax.fori_loop(0, PACK, give, 0)
        swap(p).start()

    mine = core * pairs + lax.rem(me // 2, pairs)
    home = mine * EXPERTS + me // group
    give_piece(0)
    for p, (off, w) in enumerate(returns):
        lanes = pl.ds(off, w)
        if p + 1 < len(returns):
            give_piece(p + 1)
        swap(p).wait_recv()

        def keep(c, _):
            at = some_rows(c)
            total = down(core, c, off, w).astype(BF16).astype(F32) + yrecv[at, lanes].astype(F32)
            ystack[at, lanes] = total.astype(BF16)
            return 0

        lax.fori_loop(0, PACK, keep, 0)

        def pack(b, _):
            stack = jnp.concatenate(
                [
                    ystack[pl.ds(pl.multiple_of(c * rows + b * 64, 64), 64), lanes]
                    for c in range(PACK)
                ],
                axis=0,
            )
            packed[pl.ds(pl.multiple_of(b * span, span), span), lanes] = dot(
                perm[1], stack
            ).astype(BF16)
            return 0

        lax.fori_loop(0, blocks, pack, 0)

        def give_back(i, _):
            target = lax.rem(me + i, n)
            remote(
                packed.at[at16(target), lanes],
                back.at[at16(home), lanes],
                b_send.at[p],
                b_recv.at[p],
                target,
            ).start()
            return 0

        lax.fori_loop(1, n, give_back, 0)
        back[at16(home), lanes] = packed[at16(me), lanes]

    for p, (off, w) in enumerate(returns):
        all_rows(packed, off, w, b_recv.at[p]).wait()
        for h in range(2):
            total = jnp.zeros((64, w), F32)
            for k in range(pairs):
                start = (h * pairs + k) * EXPERTS * ROWS
                total += dot(gated_place[...], back[start : start + EXPERTS * ROWS, off : off + w])
            total = total[0:32] + total[32:64]
            for c in range(PACK):
                start = h * half + c * quarter + off
                value = stream[:, start : start + w] + total[c * 8 : c * 8 + 8]
                value = value.astype(BF16)
                out[0, :, start : start + w] = value[0:4]
                out[1, :, start : start + w] = value[4:8]

    for p, (off, w) in enumerate(pieces):
        all_rows(packed, off, w, d_send.at[p]).wait()
        forward(p).wait_send()
    for p, (off, w) in enumerate(returns):
        swap(p).wait_send()
        all_rows(packed, off, w, b_send.at[p]).wait()


def on_device(hidden_in, norm_gain, router, expert_ids, w_gate, w_up, w_down):
    n = lax.axis_size("expert")
    width = hidden_in.shape[2]
    units = w_gate.shape[2]
    quarter = width // 2 // PACK
    pieces = cut(quarter, DISPATCH)
    returns = cut(quarter, RETURN)
    widest = max(w for _, w in pieces)
    rows = n * 4
    vmem = pl.BlockSpec(memory_space=pltpu.VMEM)
    hbm = pl.BlockSpec(memory_space=pl.ANY)
    sems = [pltpu.SemaphoreType.DMA((len(pieces),))] * 4
    sems += [pltpu.SemaphoreType.DMA((len(returns),))] * 4
    return pl.pallas_call(
        functools.partial(kernel, n, pieces, returns),
        out_shape=jax.ShapeDtypeStruct(hidden_in.shape, BF16),
        in_specs=[vmem] * 4 + [hbm] * 3,
        out_specs=vmem,
        scratch_shapes=[
            pltpu.VMEM((width, units), BF16),
            pltpu.VMEM((width, units), BF16),
            pltpu.VMEM((units, width), BF16),
            pltpu.VMEM((8, width), F32),
            pltpu.VMEM((8, width), F32),
            pltpu.VMEM((2, EXPERTS * ROWS, quarter), BF16),
            pltpu.VMEM((2, n * ROWS, quarter), BF16),
            pltpu.VMEM((PACK, rows, widest), BF16),
            pltpu.VMEM((2, SENDERS * ROWS, SENDERS * ROWS), BF16),
            pltpu.VMEM((rows, units), F32),
            pltpu.VMEM((rows, units), F32),
            pltpu.VMEM((rows, units), BF16),
            pltpu.VMEM((PACK * rows, quarter), BF16),
            pltpu.VMEM((PACK * rows, quarter), BF16),
            pltpu.VMEM((PACK * rows, quarter), BF16),
            pltpu.VMEM((n * ROWS, quarter), BF16),
            pltpu.VMEM((n * ROWS, quarter), BF16),
            pltpu.VMEM((64, EXPERTS * ROWS), BF16),
            pltpu.SemaphoreType.DMA((5,)),
        ]
        + sems,
        compiler_params=pltpu.CompilerParams(
            collective_id=0, has_side_effects=True, vmem_limit_bytes=60 * 2**20
        ),
    )(
        hidden_in,
        norm_gain.reshape(1, width),
        router.T,
        expert_ids.transpose(0, 2, 1),
        w_gate,
        w_up,
        w_down,
    )


def solution(mesh):
    placed = (
        P(None, ("replica", "expert"), None),
        P(),
        P(),
        P(None, ("replica", "expert"), None),
        P("expert", None, None),
        P("expert", None, None),
        P("expert", None, None),
    )
    return jax.shard_map(
        on_device,
        mesh=mesh,
        in_specs=placed,
        out_specs=P(None, ("replica", "expert"), None),
        check_vma=False,
    )
```

```python
import functools

import jax
import jax.numpy as jnp
from jax import lax
from jax.experimental import pallas as pl
from jax.experimental.pallas import tpu as pltpu
from jax.sharding import PartitionSpec as P

EXPERTS = 8
PACK = 4
ROWS = 16
SENDERS = 16
DISPATCH = (4, 3)
RETURN = (2, 2, 3)
F32 = jnp.float32
BF16 = jnp.bfloat16


def cut(columns, shares):
    units, total = columns // 128, sum(shares)
    ends = [units * sum(shares[: k + 1]) // total * 128 for k in range(len(shares))]
    starts = [0] + ends[:-1]
    return tuple((a, b - a) for a, b in zip(starts, ends) if b > a)


def dot(a, b, precision=None):
    return jnp.dot(a, b, preferred_element_type=F32, precision=precision)


def iota(shape, dim):
    return lax.broadcasted_iota(jnp.int32, shape, dim)


def kernel(
    n,
    pieces,
    returns,
    hid,
    gain,
    router,
    ids,
    wg_hbm,
    wu_hbm,
    wd_hbm,
    out,
    wg,
    wu,
    wd,
    stream,
    normed,
    outbox,
    arr,
    xs,
    perm,
    gate_acc,
    up_acc,
    inner,
    ysend,
    yrecv,
    ystack,
    packed,
    back,
    gated_place,
    w_sem,
    d_send,
    d_recv,
    f_send,
    f_recv,
    y_send,
    y_recv,
    b_send,
    b_recv,
):
    me = lax.axis_index("expert")
    core = lax.rem(me, 2)
    other = 1 - core
    partner = me + 1 - 2 * core
    group = n // EXPERTS
    pairs = group // 2
    width = hid.shape[2]
    half = width // 2
    quarter = half // PACK
    rows = n * 4
    blocks = n // SENDERS

    def weight_copy(src, dst, h, sem):
        at = pl.ds(pl.multiple_of(h * half, 128), half)
        return pltpu.make_async_copy(src.at[0, at, :], dst.at[at, :], w_sem.at[sem])

    copies = [
        weight_copy(wg_hbm, wg, core, 0),
        weight_copy(wu_hbm, wu, core, 1),
        weight_copy(wg_hbm, wg, other, 2),
        weight_copy(wu_hbm, wu, other, 3),
        pltpu.make_async_copy(wd_hbm.at[0], wd, w_sem.at[4]),
    ]
    for copy in copies:
        copy.start()

    barrier = pltpu.get_barrier_semaphore()

    def greet(i, _):
        pl.semaphore_signal(
            barrier,
            inc=1,
            device_id={"expert": lax.rem(me + i, n)},
            device_id_type=pl.DeviceIdType.MESH,
        )
        return 0

    lax.fori_loop(1, n, greet, 0)

    x = jnp.concatenate([hid[0].astype(F32), hid[1].astype(F32)], axis=0)
    stream[...] = x
    scale = lax.rsqrt(jnp.mean(x * x, axis=-1, keepdims=True) + 1e-06)
    y = x * scale * gain[...]
    normed[...] = y

    diagonal = iota((4, 4), 0) == iota((4, 4), 1)

    def choice(k):
        return jnp.concatenate(
            [
                jnp.sum(
                    jnp.where(diagonal, ids[m, k : k + 1, :].astype(F32), 0.0),
                    axis=1,
                    keepdims=True,
                )
                for m in range(2)
            ],
            axis=0,
        )

    col = iota((8, 128), 1)
    expert = (col // ROWS).astype(F32)
    member = jnp.where((choice(0) == expert) | (choice(1) == expert), 1.0, 0.0).astype(F32)
    r8, c8 = iota((8, 8), 0), iota((8, 8), 1)
    earlier = jnp.where((c8 < r8) & (c8 // 4 == r8 // 4), 1.0, 0.0).astype(F32)
    position = dot(earlier, member)
    token = iota((8, 128), 0)
    slot = lax.rem(col, 4) - 2 * (token // 4)
    place = jnp.where(position == slot.astype(F32), member, 0.0)
    piece = lax.rem(col // 4, PACK)
    spread = jnp.concatenate([jnp.where(piece == c, place, 0.0) for c in range(PACK)], axis=0)
    spread_t = spread.T.astype(BF16)
    for h in range(2):
        stack = jnp.concatenate(
            [
                normed[:, h * half + c * quarter : h * half + (c + 1) * quarter]
                for c in range(PACK)
            ],
            axis=0,
        ).astype(BF16)
        outbox[h] = dot(spread_t, stack).astype(BF16)

    pl.semaphore_wait(barrier, n - 1)

    def remote(src, dst, send, recv, target):
        return pltpu.make_async_remote_copy(
            src_ref=src,
            dst_ref=dst,
            send_sem=send,
            recv_sem=recv,
            device_id={"expert": target},
            device_id_type=pl.DeviceIdType.MESH,
        )

    def at16(index):
        return pl.ds(pl.multiple_of(index * ROWS, ROWS), ROWS)

    for p, (off, w) in enumerate(pieces):
        lanes = pl.ds(off, w)

        def dispatch(i, _):
            target = lax.rem(me + lax.rem(i, 2) * ((i + 1) // 2) + (1 - lax.rem(i, 2)) * (n - i // 2), n)
            h = lax.rem(target, 2)
            remote(
                outbox.at[h, at16(target // group), lanes],
                arr.at[h, at16(me), lanes],
                d_send.at[p],
                d_recv.at[p],
                target,
            ).start()
            return 0

        lax.fori_loop(1, n, dispatch, 0)
    arr[core, at16(me), :] = outbox[core, at16(me // group), :]

    logits = lax.dot_general(
        normed[...],
        router[...],
        (((1,), (1,)), ((), ())),
        precision=lax.Precision.HIGHEST,
        preferred_element_type=F32,
    )
    scores = jax.nn.sigmoid(logits)
    widen = jnp.where(iota((8, 128), 0) == iota((8, 128), 1) // ROWS, 1.0, 0.0).astype(F32)
    wide = dot(scores, widen, lax.Precision.HIGHEST) * member
    gates = 2.5 * wide / (jnp.sum(wide, axis=1, keepdims=True) * (1.0 / ROWS))
    gated = spread * jnp.concatenate([gates] * PACK, axis=0)
    high = gated.astype(BF16)
    gated_place[0:32, :] = high
    gated_place[32:64, :] = (gated - high.astype(F32)).astype(BF16)

    span = SENDERS * ROWS
    r, q = iota((span, span), 0), iota((span, span), 1)

    def where_from(v):
        return lax.rem(v, 64) // 4 * ROWS + v // 64 * 4 + lax.rem(v, 4)

    perm[0] = jnp.where(where_from(r) == q, 1.0, 0.0).astype(BF16)
    perm[1] = jnp.where(where_from(q) == r, 1.0, 0.0).astype(BF16)
    gate_acc[...] = jnp.zeros_like(gate_acc)
    up_acc[...] = jnp.zeros_like(up_acc)

    def hidden_units(h, off, w):
        lanes = pl.ds(off, w)

        def unpack(b, _):
            z = dot(perm[0], arr[h, pl.ds(pl.multiple_of(b * span, span), span), lanes])
            z = z.astype(BF16)
            for c in range(PACK):
                xs[c, pl.ds(pl.multiple_of(b * 64, 64), 64), 0:w] = z[c * 64 : c * 64 + 64]
            return 0

        lax.fori_loop(0, blocks, unpack, 0)

        def add(c, _):
            depth = pl.ds(pl.multiple_of(h * half + c * quarter + off, 128), w)
            part = xs[c, :, 0:w]
            gate_acc[...] += dot(part, wg[depth, :])
            up_acc[...] += dot(part, wu[depth, :])
            return 0

        lax.fori_loop(0, PACK, add, 0)

    def all_rows(ref, off, w, sem):
        at = ref.at[pl.ds(0, (n - 1) * ROWS), pl.ds(off, w)]
        return pltpu.make_async_copy(at, at, sem)

    def forward(p):
        off, w = pieces[p]
        at = arr.at[core, :, pl.ds(off, w)]
        return remote(at, at, f_send.at[p], f_recv.at[p], partner)

    for p, (off, w) in enumerate(pieces):
        all_rows(packed, off, w, d_recv.at[p]).wait()
        forward(p).start()
        if p == 0:
            copies[0].wait()
            copies[1].wait()
        hidden_units(core, off, w)
        forward(p).wait_recv()
        if p == 0:
            copies[2].wait()
            copies[3].wait()
        hidden_units(other, off, w)

    g = gate_acc[...]
    inner[...] = (g / (1.0 + jnp.exp(-g)) * up_acc[...]).astype(BF16)
    copies[4].wait()

    def down(h, c, off, w):
        at = pl.ds(pl.multiple_of(h * half + c * quarter + off, 128), w)
        return dot(inner[...], wd[:, at])

    def some_rows(c):
        return pl.ds(pl.multiple_of(c * rows, 64), rows)

    def swap(p):
        off, w = returns[p]
        lanes = pl.ds(off, w)
        return remote(
            ysend.at[:, lanes], yrecv.at[:, lanes], y_send.at[p], y_recv.at[p], partner
        )

    def give_piece(p):
        off, w = returns[p]

        def give(c, _):
            ysend[some_rows(c), pl.ds(off, w)] = down(other, c, off, w).astype(BF16)
            return 0

        lax.fori_loop(0, PACK, give, 0)
        swap(p).start()

    mine = core * pairs + lax.rem(me // 2, pairs)
    home = mine * EXPERTS + me // group
    give_piece(0)
    for p, (off, w) in enumerate(returns):
        lanes = pl.ds(off, w)
        if p + 1 < len(returns):
            give_piece(p + 1)
        swap(p).wait_recv()

        def keep(c, _):
            at = some_rows(c)
            total = down(core, c, off, w).astype(BF16).astype(F32) + yrecv[at, lanes].astype(F32)
            ystack[at, lanes] = total.astype(BF16)
            return 0

        lax.fori_loop(0, PACK, keep, 0)

        def pack(b, _):
            stack = jnp.concatenate(
                [
                    ystack[pl.ds(pl.multiple_of(c * rows + b * 64, 64), 64), lanes]
                    for c in range(PACK)
                ],
                axis=0,
            )
            packed[pl.ds(pl.multiple_of(b * span, span), span), lanes] = dot(
                perm[1], stack
            ).astype(BF16)
            return 0

        lax.fori_loop(0, blocks, pack, 0)

        def give_back(i, _):
            target = lax.rem(me + lax.rem(i, 2) * ((i + 1) // 2) + (1 - lax.rem(i, 2)) * (n - i // 2), n)
            remote(
                packed.at[at16(target), lanes],
                back.at[at16(home), lanes],
                b_send.at[p],
                b_recv.at[p],
                target,
            ).start()
            return 0

        lax.fori_loop(1, n, give_back, 0)
        back[at16(home), lanes] = packed[at16(me), lanes]

    for p, (off, w) in enumerate(returns):
        all_rows(packed, off, w, b_recv.at[p]).wait()
        for h in range(2):
            total = jnp.zeros((64, w), F32)
            for k in range(pairs):
                start = (h * pairs + k) * EXPERTS * ROWS
                total += dot(gated_place[...], back[start : start + EXPERTS * ROWS, off : off + w])
            total = total[0:32] + total[32:64]
            for c in range(PACK):
                start = h * half + c * quarter + off
                value = stream[:, start : start + w] + total[c * 8 : c * 8 + 8]
                value = value.astype(BF16)
                out[0, :, start : start + w] = value[0:4]
                out[1, :, start : start + w] = value[4:8]

    for p, (off, w) in enumerate(pieces):
        all_rows(packed, off, w, d_send.at[p]).wait()
        forward(p).wait_send()
    for p, (off, w) in enumerate(returns):
        swap(p).wait_send()
        all_rows(packed, off, w, b_send.at[p]).wait()


def on_device(hidden_in, norm_gain, router, expert_ids, w_gate, w_up, w_down):
    n = lax.axis_size("expert")
    width = hidden_in.shape[2]
    units = w_gate.shape[2]
    quarter = width // 2 // PACK
    pieces = cut(quarter, DISPATCH)
    returns = cut(quarter, RETURN)
    widest = max(w for _, w in pieces)
    rows = n * 4
    vmem = pl.BlockSpec(memory_space=pltpu.VMEM)
    hbm = pl.BlockSpec(memory_space=pl.ANY)
    sems = [pltpu.SemaphoreType.DMA((len(pieces),))] * 4
    sems += [pltpu.SemaphoreType.DMA((len(returns),))] * 4
    return pl.pallas_call(
        functools.partial(kernel, n, pieces, returns),
        out_shape=jax.ShapeDtypeStruct(hidden_in.shape, BF16),
        in_specs=[vmem] * 4 + [hbm] * 3,
        out_specs=vmem,
        scratch_shapes=[
            pltpu.VMEM((width, units), BF16),
            pltpu.VMEM((width, units), BF16),
            pltpu.VMEM((units, width), BF16),
            pltpu.VMEM((8, width), F32),
            pltpu.VMEM((8, width), F32),
            pltpu.VMEM((2, EXPERTS * ROWS, quarter), BF16),
            pltpu.VMEM((2, n * ROWS, quarter), BF16),
            pltpu.VMEM((PACK, rows, widest), BF16),
            pltpu.VMEM((2, SENDERS * ROWS, SENDERS * ROWS), BF16),
            pltpu.VMEM((rows, units), F32),
            pltpu.VMEM((rows, units), F32),
            pltpu.VMEM((rows, units), BF16),
            pltpu.VMEM((PACK * rows, quarter), BF16),
            pltpu.VMEM((PACK * rows, quarter), BF16),
            pltpu.VMEM((PACK * rows, quarter), BF16),
            pltpu.VMEM((n * ROWS, quarter), BF16),
            pltpu.VMEM((n * ROWS, quarter), BF16),
            pltpu.VMEM((64, EXPERTS * ROWS), BF16),
            pltpu.SemaphoreType.DMA((5,)),
        ]
        + sems,
        compiler_params=pltpu.CompilerParams(
            collective_id=0, has_side_effects=True, vmem_limit_bytes=60 * 2**20
        ),
    )(
        hidden_in,
        norm_gain.reshape(1, width),
        router.T,
        expert_ids.transpose(0, 2, 1),
        w_gate,
        w_up,
        w_down,
    )


def solution(mesh):
    placed = (
        P(None, ("replica", "expert"), None),
        P(),
        P(),
        P(None, ("replica", "expert"), None),
        P("expert", None, None),
        P("expert", None, None),
        P("expert", None, None),
    )
    return jax.shard_map(
        on_device,
        mesh=mesh,
        in_specs=placed,
        out_specs=P(None, ("replica", "expert"), None),
        check_vma=False,
    )
```
